32 devices in a mesh: row: 8 (over y, x, core), col: 4 (over z).
Axes of the slice: x: 2, y: 2, z: 4, core: 2. Of those that a mesh axis runs over, the one named last changes fastest.
Arguments:
- tiles: bfloat16 [8, 4, 128, 128, 128], P('row', 'col'), as said below
- coords: int32 [8, 4, 2, 128], P('row', 'col'), may hold values from 0 to 31, as said below
- counts: int32 [8, 4], P('row', 'col'), may hold values from 1 to 128, as said below
- valid: int32 [16384], P(('row', 'col')), may hold values 0 or 1
- start: float32 [8, 16384], P(None, ('row', 'col'))
- rotations: float32 [2, 8, 24], replicated, as said below
Outputs:
- eigenmaps: float32 [8, 16384], P(None, ('row', 'col'))
- ritz: float32 [8, 8], replicated
The draws below stay inside these ranges and needn't reach their ends.
Inputs may be any that keep to these rules, and one draw needn't show every extreme that they name: coords[r, c, 0, s] is a block row from 0 to 15 and coords[r, c, 1, s] a block column from 0 to 31; the live slots of one owner name distinct blocks, each on or above the block diagonal (g_row <= g_col). The live slots of an owner are the first counts[r, c] of its list; one owner in grid row 0 has all 128 live. `tiles`: nonnegative; a tile on the block diagonal is symmetric. The Rayleigh-Ritz coefficients of the current vectors, rotations[t, :, 0 to 7], form a matrix whose diagonal dominates its rows.
All inputs are finite; a program needn't handle non-finite values. No bound on the sum of `valid` on one device may be relied on, other than what follows from the above.
Results may differ from the reference program's by a relative error of at most 0.0013.
Values may be sent and summed in bfloat16 or wider, within the bound.
A program may use at most 64 MiB of HBM per device.

```python
import math
import jax
import jax.numpy as jnp
from jax import lax

TILE = 128
VECS = 8
ITERS = 2
STRETCH = 512
SLOTS = 128
NODES = 16384
BLOCKS = 128
N_ROW = 8
N_COL = 4


def owner_layout(key):
    per_stretch = STRETCH // TILE
    row_span = N_COL * per_stretch
    col_span = N_ROW * per_stretch
    cells = row_span * col_span
    cell_index = jnp.arange(cells, dtype=jnp.int32)
    block_rows = cell_index // col_span
    block_cols = cell_index % col_span
    row_owner = jnp.arange(N_ROW, dtype=jnp.int32)[:, None, None]
    col_owner = jnp.arange(N_COL, dtype=jnp.int32)[None, :, None]
    global_rows = row_owner * row_span + block_rows[None, None, :]
    global_cols = (block_cols[None, None, :] // per_stretch * N_COL + col_owner) * per_stretch + block_cols[None, None, :] % per_stretch
    upper = global_rows <= global_cols
    spread = 2 ** 30 // cells
    noise = jax.random.randint(jax.random.fold_in(key, 1), (N_ROW, N_COL, cells), 0, spread, dtype=jnp.int32)
    score = noise * cells + cell_index[None, None, :] + jnp.where(upper, 0, 2 ** 30).astype(jnp.int32)
    score = jnp.where(cell_index[None, None, :] == col_span - 1, -1, score).astype(jnp.int32)
    chosen = jnp.argsort(score, axis=-1, stable=True)[..., :SLOTS].astype(jnp.int32)
    coords = jnp.stack([chosen // col_span, chosen % col_span], axis=2).astype(jnp.int32)
    available = jnp.sum(upper.astype(jnp.int32), axis=-1)
    divisor = 1 + jax.random.randint(jax.random.fold_in(key, 2), (N_ROW, N_COL), 0, 5, dtype=jnp.int32)
    wanted = jnp.maximum(1, SLOTS // divisor)
    full_col = jax.random.randint(jax.random.fold_in(key, 3), (), 0, N_COL, dtype=jnp.int32)
    is_full = (jnp.arange(N_ROW, dtype=jnp.int32)[:, None] == 0) & (jnp.arange(N_COL, dtype=jnp.int32)[None, :] == full_col)
    wanted = jnp.where(is_full, SLOTS, wanted)
    counts = jnp.minimum(wanted, available).astype(jnp.int32)
    return (coords, counts)


def draw_coords(key, part):
    return owner_layout(jax.random.fold_in(key, 7))[0]


def draw_counts(key, part):
    return owner_layout(jax.random.fold_in(key, 7))[1]


def draw_tiles(key, part):
    coords, counts = owner_layout(jax.random.fold_in(key, 7))
    per_stretch = STRETCH // TILE
    row_span = N_COL * per_stretch
    row_owner = jnp.arange(N_ROW, dtype=jnp.int32)[:, None, None]
    col_owner = jnp.arange(N_COL, dtype=jnp.int32)[None, :, None]
    global_rows = row_owner * row_span + coords[:, :, 0, :]
    global_cols = (coords[:, :, 1, :] // per_stretch * N_COL + col_owner) * per_stretch + coords[:, :, 1, :] % per_stretch
    on_diagonal = global_rows == global_cols
    shape = (N_ROW, N_COL, SLOTS, TILE, TILE)
    total_live = jnp.sum(counts).astype(jnp.float32)
    tiles_per_block = 2.0 * total_live / BLOCKS
    keep_share = jnp.minimum(1.0, 16.0 / (TILE * tiles_per_block))
    keep = jax.random.uniform(jax.random.fold_in(key, 12), shape, jnp.float32) < keep_share
    base = jnp.exp(-3.0 * jax.random.uniform(jax.random.fold_in(key, 11), shape, jnp.float32))
    weights = jnp.where(keep, base, 0.0) * 0.125
    mirrored = 0.5 * (weights + jnp.swapaxes(weights, -1, -2))
    weights = jnp.where(on_diagonal[..., None, None], mirrored, weights)
    return weights.astype(jnp.bfloat16)


def draw_start(key, part):
    positions = jnp.arange(NODES, dtype=jnp.float32) / NODES
    rising = jnp.exp(math.log(3.0) * positions)[None, :]
    values = jax.random.normal(jax.random.fold_in(key, 21), (VECS, NODES), jnp.float32)
    return (values * rising).astype(jnp.float32)


def draw_rotations(key, part):
    shape = (ITERS, VECS, 3 * VECS)
    row_at = jnp.arange(VECS, dtype=jnp.int32)[None, :, None]
    col_at = jnp.arange(3 * VECS, dtype=jnp.int32)[None, None, :]
    spread = jax.random.uniform(jax.random.fold_in(key, 31), shape, jnp.float32, -1.0, 1.0)
    normal_part = jax.random.normal(jax.random.fold_in(key, 32), shape, jnp.float32)
    leading = jnp.where(row_at == col_at, 1.0, 0.12 * spread)
    return jnp.where(col_at < VECS, leading, 0.5 * normal_part).astype(jnp.float32)


def set_ends(values, rng, low, high):
    longest = values.shape.index(max(values.shape))
    spots = []
    for shift in (0, 1):
        where = [jax.random.randint(jax.random.fold_in(rng, axis), (), 0, length) for axis, length in enumerate(values.shape)]
        where[longest] = (where[longest] + shift) % values.shape[longest]
        spots.append(tuple(where))
    return values.at[spots[0]].set(low).at[spots[1]].set(high)


def setup_inputs(seed: int = 0) -> dict:
    key_list = jax.random.split(jax.random.key(seed), 7)
    return {
        "tiles": draw_tiles(jax.random.fold_in(key_list[6], 71), 0),
        "coords": draw_coords(jax.random.fold_in(key_list[6], 71), 0),
        "counts": draw_counts(jax.random.fold_in(key_list[6], 71), 0),
        "valid": set_ends((jax.random.randint(key_list[3], (NODES,), 0, 8) < 7).astype(jnp.int32), jax.random.fold_in(key_list[3], 1), 0, 1),
        "start": draw_start(jax.random.fold_in(key_list[6], 71), 0),
        "rotations": draw_rotations(jax.random.fold_in(key_list[6], 71), 0),
    }


def matmul_high(left, right):
    return jnp.dot(left, right, precision=lax.Precision.HIGHEST)

def lower_inverse(lower_factor):
    order_size = lower_factor.shape[0]
    identity = jnp.eye(order_size, dtype=lower_factor.dtype)
    inverse_rows = []
    for row_at in range(order_size):
        partial_row = identity[row_at]
        for prior_at in range(row_at):
            partial_row = partial_row - lower_factor[row_at, prior_at] * inverse_rows[prior_at]
        inverse_rows.append(partial_row / lower_factor[row_at, row_at])
    return jnp.stack(inverse_rows)

def settle(new_vecs, new_images, new_steps, step_images, gram_x, gram_ax):
    node_total = jnp.float32(NODES)
    lower_factor = jnp.linalg.cholesky(gram_x / node_total)
    inverse = lower_inverse(lower_factor)
    theta = matmul_high(matmul_high(inverse, gram_ax / node_total), inverse.T)
    return (matmul_high(inverse, new_vecs), matmul_high(inverse, new_images), matmul_high(inverse, new_steps), matmul_high(inverse, step_images), theta)

def graph_product(vectors, tiles, coords, counts):
    width = vectors.shape[0]
    per_stretch = STRETCH // TILE
    row_span = N_COL * per_stretch
    owners = N_ROW * N_COL
    blocks = vectors.reshape(width, BLOCKS, TILE)
    flat_tiles = tiles.reshape(owners, SLOTS, TILE, TILE)
    flat_coords = coords.reshape(owners, 2, SLOTS)
    flat_counts = counts.reshape(owners)

    def visit(total, inputs):
        owner_tiles, owner_coords, owner_count, owner_id = inputs
        row_owner = owner_id // N_COL
        col_owner = owner_id % N_COL
        block_rows = owner_coords[0]
        block_cols = owner_coords[1]
        global_rows = row_owner * row_span + block_rows
        global_cols = (block_cols // per_stretch * N_COL + col_owner) * per_stretch + block_cols % per_stretch
        live = (jnp.arange(SLOTS, dtype=jnp.int32) < owner_count).astype(jnp.float32)
        mirror_weight = live * (global_rows != global_cols).astype(jnp.float32)
        dense = owner_tiles.astype(jnp.float32)
        col_values = blocks[:, global_cols].astype(jnp.float32)
        row_values = blocks[:, global_rows].astype(jnp.float32)
        direct = jnp.einsum('sut,cst->csu', dense, col_values, precision=lax.Precision.HIGHEST) * live[None, :, None]
        mirror = jnp.einsum('sut,csu->cst', dense, row_values, precision=lax.Precision.HIGHEST) * mirror_weight[None, :, None]
        total = total.at[:, global_rows].add(direct).at[:, global_cols].add(mirror)
        return (total, None)
    start_total = jnp.zeros((width, BLOCKS, TILE), jnp.float32)
    total = lax.scan(visit, start_total, (flat_tiles, flat_coords, flat_counts, jnp.arange(owners, dtype=jnp.int32)))[0]
    return total.reshape(width, NODES)

def reference(tiles, coords, counts, valid, start, rotations):
    node_mask = valid.astype(jnp.float32)
    first_vecs = start * node_mask[None, :]
    probe = jnp.concatenate([node_mask[None, :], first_vecs], 0).astype(jnp.bfloat16)
    raw = graph_product(probe, tiles, coords, counts)
    degree = raw[0]
    first_images = node_mask[None, :] * (degree[None, :] * first_vecs - raw[1:])
    zero_steps = jnp.zeros_like(first_vecs)
    vecs, images, steps, step_images, theta = settle(first_vecs, first_images, zero_steps, zero_steps, matmul_high(first_vecs, first_vecs.T), matmul_high(first_images, first_vecs.T))
    for turn in range(ITERS):
        resid = images - matmul_high(theta, vecs)
        resid_images = node_mask[None, :] * (degree[None, :] * resid - graph_product(resid.astype(jnp.bfloat16), tiles, coords, counts))
        stacked = jnp.concatenate([vecs, resid, steps], 0)
        stacked_images = jnp.concatenate([images, resid_images, step_images], 0)
        rotation = rotations[turn]
        new_vecs = matmul_high(rotation, stacked)
        new_images = matmul_high(rotation, stacked_images)
        new_steps = matmul_high(rotation[:, VECS:], stacked[VECS:])
        new_step_images = matmul_high(rotation[:, VECS:], stacked_images[VECS:])
        vecs, images, steps, step_images, theta = settle(new_vecs, new_images, new_steps, new_step_images, matmul_high(new_vecs, new_vecs.T), matmul_high(new_images, new_vecs.T))
    return (vecs, theta)
```

```python
import functools
import jax
import jax.numpy as jnp
from jax import lax
from jax.experimental import pallas as pl
from jax.experimental.pallas import tpu as pltpu
from jax.sharding import PartitionSpec as P

F32 = jnp.float32
BF16 = jnp.bfloat16
MESH = pl.DeviceIdType.MESH
UNROLL = 8


def dot_high(left, right):
    return jnp.dot(left, right, precision=lax.Precision.HIGHEST, preferred_element_type=F32)


def dot_lanes(left, right, precision=None):
    return lax.dot_general(
        left, right, (((1,), (1,)), ((), ())), precision=precision, preferred_element_type=F32
    )


def split(values):
    high = values.astype(BF16)
    return high, (values - high.astype(F32)).astype(BF16)


def inverse_lower(gram):
    size = gram.shape[0]
    rows = lax.broadcasted_iota(jnp.int32, (size, size), 0)
    cols = lax.broadcasted_iota(jnp.int32, (size, size), 1)
    diag = rows == cols
    work = gram
    made = jnp.where(diag, 1.0, 0.0).astype(F32)
    for k in range(size - 1):
        column = work[:, k : k + 1]
        factor = jnp.where(rows[:, :1] > k, column / work[k : k + 1, k : k + 1], 0.0)
        work, made = work - factor * work[k : k + 1, :], made - factor * made[k : k + 1, :]
    pivots = jnp.sum(jnp.where(diag, work, 0.0), axis=1, keepdims=True)
    return made * lax.rsqrt(pivots)


def kernel(
    n_row, n_col, turns,
    tiles_hbm, places, places_vec, counts, valid, start, rotations,
    maps_out, ritz_out,
    tiles, pick_rows, pick_cols, direct, mirror, rows_total, cols_total,
    col_vecs, row_vecs, row_land, col_land, gram_row, gram_col,
    tile_sem, send_vec, recv_vec, send_sum, recv_sum, send_gram, recv_gram,
):
    me_row = lax.axis_index("row")
    me_col = lax.axis_index("col")
    slots, side, _ = tiles.shape
    count, stretch = start.shape
    per = stretch // side
    node_total = float(stretch * n_row * n_col)
    chunk = per * count

    fetch = pltpu.make_async_copy(tiles_hbm, tiles, tile_sem)
    fetch.start()

    def row_peer(d):
        return (lax.rem(me_row + d, n_row), me_col)

    def col_peer(d):
        return (me_row, lax.rem(me_col + d, n_col))

    peers = [("row", d) for d in range(1, n_row)] + [("col", d) for d in range(1, n_col)]
    barrier = pltpu.get_barrier_semaphore()
    for axis, d in peers:
        where = row_peer(d) if axis == "row" else col_peer(d)
        pl.semaphore_signal(barrier, inc=1, device_id=where, device_id_type=MESH)

    mask = valid[...].astype(F32)
    first = start[...] * mask

    def put_vectors(turn, top, bottom):
        both = jnp.concatenate([top, bottom], axis=0).astype(BF16)
        for k in range(per):
            part = both[:, k * side : (k + 1) * side]
            col_vecs[turn, me_row * per + k] = part
            row_vecs[turn, me_col * per + k] = part

    def vector_copies(turn):
        copies = []
        for at, (axis, d) in enumerate(peers):
            buffer, mine, where = (
                (col_vecs, me_row, row_peer(d)) if axis == "row" else (row_vecs, me_col, col_peer(d))
            )
            span = buffer.at[turn, pl.ds(mine * per, per)]
            copies.append(
                pltpu.make_async_remote_copy(
                    src_ref=span, dst_ref=span,
                    send_sem=send_vec.at[turn, at], recv_sem=recv_vec.at[turn, at],
                    device_id=where, device_id_type=MESH,
                )
            )
        return copies

    def sum_copies(turn, wide):
        copies = []
        height = chunk * (2 if wide else 1)
        for at, (axis, d) in enumerate(peers):
            total, land, there, where = (
                (cols_total, row_land, lax.rem(me_row + d, n_row), row_peer(d))
                if axis == "row"
                else (rows_total, col_land, lax.rem(me_col + d, n_col), col_peer(d))
            )
            copies.append(
                pltpu.make_async_remote_copy(
                    src_ref=total.at[turn, there, pl.ds(0, height)],
                    dst_ref=land.at[turn, d - 1, pl.ds(0, height)],
                    send_sem=send_sum.at[turn, at], recv_sem=recv_sum.at[turn, at],
                    device_id=where, device_id_type=MESH,
                )
            )
        return copies

    def gram_copies(turn, axis):
        copies = []
        for at, (name, d) in enumerate(peers):
            if name != axis:
                continue
            buffer, where = (gram_row, row_peer(d)) if axis == "row" else (gram_col, col_peer(d))
            copies.append(
                pltpu.make_async_remote_copy(
                    src_ref=buffer.at[turn, 0], dst_ref=buffer.at[turn, d],
                    send_sem=send_gram.at[turn, at], recv_sem=recv_gram.at[turn, at],
                    device_id=where, device_id_type=MESH,
                )
            )
        return copies

    started = []

    def begin(copies):
        for copy in copies:
            copy.start()
        started.extend(copies)
        return copies

    def arrive(copies):
        for copy in copies:
            copy.wait_recv()

    put_vectors(0, first, jnp.concatenate([mask, jnp.zeros((count - 1, stretch), F32)], axis=0))
    pl.semaphore_wait(barrier, len(peers))
    vec_moves = begin(vector_copies(0))

    spread = (
        lax.broadcasted_iota(jnp.int32, (slots, slots * count), 1) // count
        == lax.broadcasted_iota(jnp.int32, (slots, slots * count), 0)
    ).astype(F32).astype(BF16)
    at_rows = places_vec[0:1, :]
    at_cols = places_vec[1:2, :]
    slot_at = lax.broadcasted_iota(jnp.int32, (1, slots), 1)
    live = slot_at < counts[0, 0]
    whole_rows = me_row * (n_col * per) + at_rows
    whole_cols = (at_cols // per * n_col + me_col) * per + at_cols % per
    key_rows = jnp.where(live, at_rows, -1).astype(F32)
    key_cols = jnp.where(live & (whole_rows != whole_cols), at_cols, -1).astype(F32)
    keys = jnp.concatenate([key_rows, key_cols, jnp.zeros((14, slots), F32)], axis=0).astype(BF16)
    wide_keys = jnp.dot(keys, spread, preferred_element_type=F32)
    lane = (lax.broadcasted_iota(jnp.int32, (1, slots * count), 1) % count).astype(F32)
    for pick, wide_key in ((pick_rows, wide_keys[0:1]), (pick_cols, wide_keys[1:2])):
        wanted = wide_key * float(count) + lane
        for low in range(0, pick.shape[0], 64):
            row_at = (lax.broadcasted_iota(jnp.int32, (64, slots * count), 0) + low).astype(F32)
            pick[pl.ds(low, 64), :] = (row_at == wanted).astype(F32).astype(BF16)

    def local_product(turn, wide):
        def visit(step, carry):
            for more in range(UNROLL):
                slot = step * UNROLL + more
                tile = tiles[slot]
                by_col = col_vecs[turn, places[1, slot]]
                by_row = row_vecs[turn, places[0, slot]]
                forth = dot_lanes(by_col, tile)
                back = jnp.dot(by_row, tile, preferred_element_type=F32)
                at = pl.multiple_of(slot * count, count)
                if wide:
                    direct[0, pl.ds(at, count), :] = forth[:count]
                    direct[1, pl.ds(at, count), :] = forth[count:]
                    mirror[0, pl.ds(at, count), :] = back[:count]
                    mirror[1, pl.ds(at, count), :] = back[count:]
                else:
                    direct[0, pl.ds(at, count), :] = forth[:count] + forth[count:]
                    mirror[0, pl.ds(at, count), :] = back[:count] + back[count:]
            return carry

        lax.fori_loop(0, slots // UNROLL, visit, 0)
        for pick, terms, total, groups in (
            (pick_rows, direct, rows_total, n_col), (pick_cols, mirror, cols_total, n_row)
        ):
            for half in range(2 if wide else 1):
                high, low = split(terms[half])
                summed = jnp.dot(pick[...], high, preferred_element_type=F32)
                summed = summed + jnp.dot(pick[...], low, preferred_element_type=F32)
                for group in range(groups):
                    total[turn, group, pl.ds(half * chunk, chunk), :] = summed[
                        group * chunk : (group + 1) * chunk
                    ]

    def collect(turn, half):
        span = pl.ds(half * chunk, chunk)
        total = rows_total[turn, me_col, span, :] + cols_total[turn, me_row, span, :]
        for d in range(1, n_col):
            total = total + col_land[turn, d - 1, span, :]
        for d in range(1, n_row):
            total = total + row_land[turn, d - 1, span, :]
        return jnp.concatenate([total[k * count : (k + 1) * count] for k in range(per)], axis=1)

    def gram_begin(turn, vecs, images):
        both = jnp.concatenate([vecs, images], axis=0)
        gram_row[turn, 0] = jnp.zeros(gram_row.shape[2:], F32)
        gram_row[turn, 0, :, 0:count] = dot_lanes(both, vecs, lax.Precision.HIGHEST)
        return begin(gram_copies(turn, "row"))

    def gram_cross(turn, moves):
        arrive(moves)
        total = jnp.zeros(gram_row.shape[2:], F32)
        for r in range(n_row):
            total = total + gram_row[turn, lax.rem(me_row - r + n_row, n_row)]
        gram_col[turn, 0] = total
        return begin(gram_copies(turn, "col"))

    def gram_end(turn, moves):
        arrive(moves)
        total = jnp.zeros(gram_col.shape[2:], F32)
        for c in range(n_col):
            total = total + gram_col[turn, lax.rem(me_col - c + n_col, n_col)]
        total = total / node_total
        inverse = inverse_lower(total[:count, :count])
        theta = dot_lanes(dot_high(inverse, total[count:, :count]), inverse, lax.Precision.HIGHEST)
        return inverse, theta

    fetch.wait()
    arrive(vec_moves)
    local_product(0, True)
    arrive(begin(sum_copies(0, True)))
    product = collect(0, 0)
    degree = collect(0, 1)[0:1]
    vecs, images = first, mask * (degree * first - product)
    steps = step_images = None
    for turn in range(turns):
        high = images.astype(BF16).astype(F32)
        put_vectors(turn + 1, high, images - high)
        vec_moves = begin(vector_copies(turn + 1))
        gram_moves = gram_begin(turn, vecs, images)
        arrive(vec_moves)
        local_product(turn + 1, False)
        sum_moves = begin(sum_copies(turn + 1, False))
        gram_moves = gram_cross(turn, gram_moves)
        inverse, theta = gram_end(turn, gram_moves)
        parts = [vecs, images] + ([] if steps is None else [steps, step_images])
        settled = dot_high(inverse, jnp.concatenate(parts, axis=1))
        pair = settled[:, : 2 * stretch]
        turned = dot_high(theta, pair)
        resid = pair[:, stretch:] - turned[:, :stretch]
        rotation = rotations[turn]
        arrive(sum_moves)
        twice = mask * (degree * images - collect(turn + 1, 0))
        resid_images = dot_high(inverse, twice) - turned[:, stretch:]
        stack = [pair, jnp.concatenate([resid, resid_images], axis=1)]
        width = 2 * count
        if steps is not None:
            stack.append(settled[:, 2 * stretch :])
            width = 3 * count
        part = rotation[:, :width]
        lanes = lax.broadcasted_iota(jnp.int32, part.shape, 1)
        lead = jnp.concatenate([part, jnp.where(lanes < count, 0.0, part)], axis=0)
        moved = dot_high(lead, jnp.concatenate(stack, axis=0))
        vecs, images = moved[:count, :stretch], moved[:count, stretch:]
        steps, step_images = moved[count:, :stretch], moved[count:, stretch:]
    gram_moves = gram_begin(turns, vecs, images)
    inverse, theta = gram_end(turns, gram_cross(turns, gram_moves))
    maps_out[...] = dot_high(inverse, vecs)
    ritz_out[...] = theta
    for copy in started:
        copy.wait_send()


def body(tiles, coords, counts, valid, start, rotations):
    n_row = lax.axis_size("row")
    n_col = lax.axis_size("col")
    slots, side = tiles.shape[2], tiles.shape[3]
    count, stretch = start.shape
    per = stretch // side
    turns = rotations.shape[0]
    phases = turns + 1
    chunk = per * count
    links = n_row + n_col - 2
    vmem = pl.BlockSpec(memory_space=pltpu.VMEM)
    smem = pl.BlockSpec(memory_space=pltpu.SMEM)
    places = coords.reshape(2, slots)
    return pl.pallas_call(
        functools.partial(kernel, n_row, n_col, turns),
        out_shape=(
            jax.ShapeDtypeStruct((count, stretch), F32),
            jax.ShapeDtypeStruct((count, count), F32),
        ),
        in_specs=[pl.BlockSpec(memory_space=pl.ANY), smem, vmem, smem, vmem, vmem, vmem],
        out_specs=(vmem, vmem),
        scratch_shapes=[
            pltpu.VMEM((slots, side, side), BF16),
            pltpu.VMEM((n_col * chunk, slots * count), BF16),
            pltpu.VMEM((n_row * chunk, slots * count), BF16),
            pltpu.VMEM((2, slots * count, side), F32),
            pltpu.VMEM((2, slots * count, side), F32),
            pltpu.VMEM((phases, n_col, 2 * chunk, side), F32),
            pltpu.VMEM((phases, n_row, 2 * chunk, side), F32),
            pltpu.VMEM((phases, n_row * per, 2 * count, side), BF16),
            pltpu.VMEM((phases, n_col * per, 2 * count, side), BF16),
            pltpu.VMEM((phases, n_row - 1, 2 * chunk, side), F32),
            pltpu.VMEM((phases, n_col - 1, 2 * chunk, side), F32),
            pltpu.VMEM((phases, n_row, 2 * count, side), F32),
            pltpu.VMEM((phases, n_col, 2 * count, side), F32),
            pltpu.SemaphoreType.DMA(()),
        ]
        + [pltpu.SemaphoreType.DMA((phases, links))] * 6,
        compiler_params=pltpu.CompilerParams(
            collective_id=0, has_side_effects=True, vmem_limit_bytes=40 * 1024 * 1024
        ),
    )(
        tiles.reshape(slots, side, side), places, places, counts,
        valid.reshape(1, stretch), start, rotations,
    )


def solution(mesh):
    in_specs = (
        P("row", "col", None, None, None),
        P("row", "col", None, None),
        P("row", "col"),
        P(("row", "col")),
        P(None, ("row", "col")),
        P(),
    )
    out_specs = (P(None, ("row", "col")), P())
    return jax.shard_map(body, mesh=mesh, in_specs=in_specs, out_specs=out_specs, check_vma=False)
```

```python
import functools
import jax
import jax.numpy as jnp
from jax import lax
from jax.experimental import pallas as pl
from jax.experimental.pallas import tpu as pltpu
from jax.sharding import PartitionSpec as P

F32 = jnp.float32
BF16 = jnp.bfloat16
MESH = pl.DeviceIdType.MESH
UNROLL = 16


def dot_high(left, right):
    return jnp.dot(left, right, precision=lax.Precision.HIGHEST, preferred_element_type=F32)


def dot_lanes(left, right, precision=None):
    return lax.dot_general(
        left, right, (((1,), (1,)), ((), ())), precision=precision, preferred_element_type=F32
    )


def mix(left, right):
    total = left[:, 0:1] * right[0:1, :]
    for k in range(1, left.shape[1]):
        total = total + left[:, k : k + 1] * right[k : k + 1, :]
    return total


def beside(first, second):
    zero = jnp.zeros_like(first)
    return jnp.concatenate(
        [jnp.concatenate([first, zero], axis=1), jnp.concatenate([zero, second], axis=1)], axis=0
    )


def split(values):
    high = values.astype(BF16)
    return high, (values - high.astype(F32)).astype(BF16)


def inverse_lower(gram):
    size = gram.shape[0]
    rows = lax.broadcasted_iota(jnp.int32, (size, size), 0)
    cols = lax.broadcasted_iota(jnp.int32, (size, size), 1)
    diag = rows == cols
    work = gram
    made = jnp.where(diag, 1.0, 0.0).astype(F32)
    for k in range(size - 1):
        column = work[:, k : k + 1]
        factor = jnp.where(rows[:, :1] > k, column / work[k : k + 1, k : k + 1], 0.0)
        work, made = work - factor * work[k : k + 1, :], made - factor * made[k : k + 1, :]
    pivots = jnp.sum(jnp.where(diag, work, 0.0), axis=1, keepdims=True)
    return made * lax.rsqrt(pivots)


def kernel(
    n_row, n_col, turns,
    tiles_hbm, places, places_vec, counts, valid, start, rotations,
    maps_out, ritz_out,
    tiles, pick_rows, pick_cols, direct, mirror, rows_total, cols_total,
    col_vecs, row_vecs, row_land, col_land, gram_row, gram_col,
    tile_sem, send_vec, recv_vec, send_sum, recv_sum, send_gram, recv_gram,
):
    me_row = lax.axis_index("row")
    me_col = lax.axis_index("col")
    slots, side, _ = tiles.shape
    count, stretch = start.shape
    per = stretch // side
    node_total = float(stretch * n_row * n_col)
    chunk = per * count

    fetch = pltpu.make_async_copy(tiles_hbm, tiles, tile_sem)
    fetch.start()

    def row_peer(d):
        return (lax.rem(me_row + d, n_row), me_col)

    def col_peer(d):
        return (me_row, lax.rem(me_col + d, n_col))

    peers = [("row", d) for d in range(1, n_row)] + [("col", d) for d in range(1, n_col)]
    barrier = pltpu.get_barrier_semaphore()
    for axis, d in peers:
        where = row_peer(d) if axis == "row" else col_peer(d)
        pl.semaphore_signal(barrier, inc=1, device_id=where, device_id_type=MESH)

    mask = valid[...].astype(F32)
    first = start[...] * mask

    def put_vectors(turn, top, bottom):
        both = jnp.concatenate([top, bottom], axis=0).astype(BF16)
        for k in range(per):
            part = both[:, k * side : (k + 1) * side]
            col_vecs[turn, me_row * per + k] = part
            row_vecs[turn, me_col * per + k] = part

    def vector_copies(turn):
        copies = []
        for at, (axis, d) in enumerate(peers):
            buffer, mine, where = (
                (col_vecs, me_row, row_peer(d)) if axis == "row" else (row_vecs, me_col, col_peer(d))
            )
            span = buffer.at[turn, pl.ds(mine * per, per)]
            copies.append(
                pltpu.make_async_remote_copy(
                    src_ref=span, dst_ref=span,
                    send_sem=send_vec.at[turn, at], recv_sem=recv_vec.at[turn, at],
                    device_id=where, device_id_type=MESH,
                )
            )
        return copies

    def sum_copies(turn, wide):
        copies = []
        height = chunk + (2 * count if wide else 0)
        for at, (axis, d) in enumerate(peers):
            total, land, there, where = (
                (cols_total, row_land, lax.rem(me_row + d, n_row), row_peer(d))
                if axis == "row"
                else (rows_total, col_land, lax.rem(me_col + d, n_col), col_peer(d))
            )
            copies.append(
                pltpu.make_async_remote_copy(
                    src_ref=total.at[turn, there, pl.ds(0, height)],
                    dst_ref=land.at[turn, d - 1, pl.ds(0, height)],
                    send_sem=send_sum.at[turn, at], recv_sem=recv_sum.at[turn, at],
                    device_id=where, device_id_type=MESH,
                )
            )
        return copies

    def gram_copies(turn, axis):
        copies = []
        for at, (name, d) in enumerate(peers):
            if name != axis:
                continue
            buffer, where = (gram_row, row_peer(d)) if axis == "row" else (gram_col, col_peer(d))
            copies.append(
                pltpu.make_async_remote_copy(
                    src_ref=buffer.at[turn, 0], dst_ref=buffer.at[turn, d],
                    send_sem=send_gram.at[turn, at], recv_sem=recv_gram.at[turn, at],
                    device_id=where, device_id_type=MESH,
                )
            )
        return copies

    started = []

    def begin(copies):
        for copy in copies:
            copy.start()
        started.extend(copies)
        return copies

    def arrive(copies):
        for copy in copies:
            copy.wait_recv()

    put_vectors(0, first, jnp.concatenate([mask, jnp.zeros((count - 1, stretch), F32)], axis=0))
    pl.semaphore_wait(barrier, len(peers))
    vec_moves = begin(vector_copies(0))

    spread = (
        lax.broadcasted_iota(jnp.int32, (slots, slots * count), 1) // count
        == lax.broadcasted_iota(jnp.int32, (slots, slots * count), 0)
    ).astype(F32).astype(BF16)
    at_rows = places_vec[0:1, :]
    at_cols = places_vec[1:2, :]
    slot_at = lax.broadcasted_iota(jnp.int32, (1, slots), 1)
    live = slot_at < counts[0, 0]
    whole_rows = me_row * (n_col * per) + at_rows
    whole_cols = (at_cols // per * n_col + me_col) * per + at_cols % per
    key_rows = jnp.where(live, at_rows, -1).astype(F32)
    key_cols = jnp.where(live & (whole_rows != whole_cols), at_cols, -1).astype(F32)
    keys = jnp.concatenate([key_rows, key_cols, jnp.zeros((14, slots), F32)], axis=0).astype(BF16)
    wide_keys = jnp.dot(keys, spread, preferred_element_type=F32)
    lane = (lax.broadcasted_iota(jnp.int32, (1, slots * count), 1) % count).astype(F32)
    for pick, wide_key in ((pick_rows, wide_keys[0:1]), (pick_cols, wide_keys[1:2])):
        wanted = wide_key * float(count) + lane
        for low in range(0, pick.shape[0], 64):
            row_at = (lax.broadcasted_iota(jnp.int32, (64, slots * count), 0) + low).astype(F32)
            pick[pl.ds(low, 64), :] = (row_at == wanted).astype(F32).astype(BF16)

    def local_product(turn, wide):
        def visit(step, carry):
            for more in range(0, UNROLL, 2):
                slot = step * UNROLL + more
                pair = tiles[pl.ds(slot, 2)].reshape(2 * side, side)
                by_col = [col_vecs[turn, places[1, slot + i]] for i in range(2)]
                by_row = [row_vecs[turn, places[0, slot + i]] for i in range(2)]
                forth = dot_lanes(jnp.concatenate(by_col, axis=0), pair)
                back = jnp.dot(beside(*by_row), pair, preferred_element_type=F32)
                for i in range(2):
                    at = pl.multiple_of((slot + i) * count, count)
                    one = forth[2 * i * count : 2 * (i + 1) * count, i * side : (i + 1) * side]
                    two = back[2 * i * count : 2 * (i + 1) * count]
                    for terms, value in ((direct, one), (mirror, two)):
                        if wide:
                            terms[0, pl.ds(at, count), :] = value[:count]
                            terms[1, pl.ds(at, count), :] = value[count:]
                        else:
                            terms[0, pl.ds(at, count), :] = value[:count] + value[count:]
            return carry

        lax.fori_loop(0, slots // UNROLL, visit, 0)
        for pick, terms, total, groups in (
            (pick_cols, mirror, cols_total, n_row), (pick_rows, direct, rows_total, n_col)
        ):
            for half in range(2 if wide else 1):
                high, low = split(terms[half])
                summed = jnp.dot(pick[...], high, preferred_element_type=F32)
                summed = summed + jnp.dot(pick[...], low, preferred_element_type=F32)
                for group in range(groups):
                    part = summed[group * chunk : (group + 1) * chunk]
                    if half == 0:
                        total[turn, group, pl.ds(0, chunk), :] = part.astype(BF16)
                        continue
                    rows = jnp.concatenate(
                        [part[k * count : k * count + 1] for k in range(per)], axis=0
                    )
                    rest = rows - rows.astype(BF16).astype(F32)
                    fill = jnp.zeros((2 * count - 2 * per, side), F32)
                    rows = jnp.concatenate([rows, rest, fill], axis=0)
                    total[turn, group, pl.ds(chunk, 2 * count), :] = rows.astype(BF16)

    def gather_sums(turn, span):
        total = rows_total[turn, me_col, span, :].astype(F32)
        total = total + cols_total[turn, me_row, span, :].astype(F32)
        for d in range(1, n_col):
            total = total + col_land[turn, d - 1, span, :].astype(F32)
        for d in range(1, n_row):
            total = total + row_land[turn, d - 1, span, :].astype(F32)
        return total

    def collect(turn):
        total = gather_sums(turn, pl.ds(0, chunk))
        return jnp.concatenate([total[k * count : (k + 1) * count] for k in range(per)], axis=1)

    def collect_degree(turn):
        total = gather_sums(turn, pl.ds(chunk, 2 * count))
        total = total[:per] + total[per : 2 * per]
        return jnp.concatenate([total[k : k + 1] for k in range(per)], axis=1)

    def gram_begin(turn, vecs, images):
        both = jnp.concatenate([vecs, images], axis=0)
        gram_row[turn, 0] = jnp.zeros(gram_row.shape[2:], F32)
        gram_row[turn, 0, :, 0:count] = dot_lanes(both, vecs, lax.Precision.HIGHEST)
        return begin(gram_copies(turn, "row"))

    def gram_cross(turn, moves):
        arrive(moves)
        total = jnp.zeros(gram_row.shape[2:], F32)
        for r in range(n_row):
            total = total + gram_row[turn, lax.rem(me_row - r + n_row, n_row)]
        gram_col[turn, 0] = total
        return begin(gram_copies(turn, "col"))

    def gram_end(turn, moves):
        arrive(moves)
        total = jnp.zeros(gram_col.shape[2:], F32)
        for c in range(n_col):
            total = total + gram_col[turn, lax.rem(me_col - c + n_col, n_col)]
        total = total / node_total
        inverse = inverse_lower(total[:count, :count])
        theta = dot_lanes(dot_high(inverse, total[count:, :count]), inverse, lax.Precision.HIGHEST)
        return inverse, theta

    fetch.wait()
    arrive(vec_moves)
    local_product(0, True)
    arrive(begin(sum_copies(0, True)))
    degree = collect_degree(0)
    vecs, images = first, mask * (degree * first - collect(0))
    steps = step_images = None
    for turn in range(turns):
        high = images.astype(BF16).astype(F32)
        put_vectors(turn + 1, high, images - high)
        vec_moves = begin(vector_copies(turn + 1))
        gram_moves = gram_begin(turn, vecs, images)
        arrive(vec_moves)
        gram_moves = gram_cross(turn, gram_moves)
        local_product(turn + 1, False)
        sum_moves = begin(sum_copies(turn + 1, False))
        inverse, theta = gram_end(turn, gram_moves)
        pair = mix(inverse, jnp.concatenate([vecs, images], axis=1))
        turned = mix(theta, pair)
        rotation = rotations[turn]
        on_vecs, on_resid = rotation[:, :count], rotation[:, count : 2 * count]
        resid = pair[:, stretch:] - turned[:, :stretch]
        moved = mix(on_resid, jnp.concatenate([resid, -turned[:, stretch:]], axis=1))
        if steps is not None:
            old = mix(inverse, jnp.concatenate([steps, step_images], axis=1))
            moved = moved + mix(rotation[:, 2 * count :], old)
        kept = mix(on_vecs, pair)
        on_twice = mix(on_resid, inverse)
        steps = moved[:, :stretch]
        vecs = kept[:, :stretch] + steps
        scaled = degree * images
        arrive(sum_moves)
        twice = mask * (scaled - collect(turn + 1))
        step_images = moved[:, stretch:] + mix(on_twice, twice)
        images = kept[:, stretch:] + step_images
    gram_moves = gram_begin(turns, vecs, images)
    inverse, theta = gram_end(turns, gram_cross(turns, gram_moves))
    maps_out[...] = mix(inverse, vecs)
    ritz_out[...] = theta
    for copy in started:
        copy.wait_send()


def body(tiles, coords, counts, valid, start, rotations):
    n_row = lax.axis_size("row")
    n_col = lax.axis_size("col")
    slots, side = tiles.shape[2], tiles.shape[3]
    count, stretch = start.shape
    per = stretch // side
    turns = rotations.shape[0]
    phases = turns + 1
    chunk = per * count
    links = n_row + n_col - 2
    vmem = pl.BlockSpec(memory_space=pltpu.VMEM)
    smem = pl.BlockSpec(memory_space=pltpu.SMEM)
    places = coords.reshape(2, slots)
    return pl.pallas_call(
        functools.partial(kernel, n_row, n_col, turns),
        out_shape=(
            jax.ShapeDtypeStruct((count, stretch), F32),
            jax.ShapeDtypeStruct((count, count), F32),
        ),
        in_specs=[pl.BlockSpec(memory_space=pl.ANY), smem, vmem, smem, vmem, vmem, vmem],
        out_specs=(vmem, vmem),
        scratch_shapes=[
            pltpu.VMEM((slots, side, side), BF16),
            pltpu.VMEM((n_col * chunk, slots * count), BF16),
            pltpu.VMEM((n_row * chunk, slots * count), BF16),
            pltpu.VMEM((2, slots * count, side), F32),
            pltpu.VMEM((2, slots * count, side), F32),
            pltpu.VMEM((phases, n_col, chunk + 2 * count, side), BF16),
            pltpu.VMEM((phases, n_row, chunk + 2 * count, side), BF16),
            pltpu.VMEM((phases, n_row * per, 2 * count, side), BF16),
            pltpu.VMEM((phases, n_col * per, 2 * count, side), BF16),
            pltpu.VMEM((phases, n_row - 1, chunk + 2 * count, side), BF16),
            pltpu.VMEM((phases, n_col - 1, chunk + 2 * count, side), BF16),
            pltpu.VMEM((phases, n_row, 2 * count, side), F32),
            pltpu.VMEM((phases, n_col, 2 * count, side), F32),
            pltpu.SemaphoreType.DMA(()),
        ]
        + [pltpu.SemaphoreType.DMA((phases, links))] * 6,
        compiler_params=pltpu.CompilerParams(
            collective_id=0, has_side_effects=True, vmem_limit_bytes=60 * 1024 * 1024
        ),
    )(
        tiles.reshape(slots, side, side), places, places, counts,
        valid.reshape(1, stretch), start, rotations,
    )


def solution(mesh):
    in_specs = (
        P("row", "col", None, None, None),
        P("row", "col", None, None),
        P("row", "col"),
        P(("row", "col")),
        P(None, ("row", "col")),
        P(),
    )
    out_specs = (P(None, ("row", "col")), P())
    return jax.shard_map(body, mesh=mesh, in_specs=in_specs, out_specs=out_specs, check_vma=False)
```

```python
import functools
import jax
import jax.numpy as jnp
from jax import lax
from jax.experimental import pallas as pl
from jax.experimental.pallas import tpu as pltpu
from jax.sharding import PartitionSpec as P

F32 = jnp.float32
BF16 = jnp.bfloat16
MESH = pl.DeviceIdType.MESH
UNROLL = 16


def dot_high(left, right):
    return jnp.dot(left, right, precision=lax.Precision.HIGHEST, preferred_element_type=F32)


def dot_lanes(left, right, precision=None):
    return lax.dot_general(
        left, right, (((1,), (1,)), ((), ())), precision=precision, preferred_element_type=F32
    )


def mix(left, right):
    total = left[:, 0:1] * right[0:1, :]
    for k in range(1, left.shape[1]):
        total = total + left[:, k : k + 1] * right[k : k + 1, :]
    return total


def beside(first, second):
    zero = jnp.zeros_like(first)
    return jnp.concatenate(
        [jnp.concatenate([first, zero], axis=1), jnp.concatenate([zero, second], axis=1)], axis=0
    )


def split(values):
    high = values.astype(BF16)
    return high, (values - high.astype(F32)).astype(BF16)


def inverse_lower(gram):
    size = gram.shape[0]
    rows = lax.broadcasted_iota(jnp.int32, (size, size), 0)
    cols = lax.broadcasted_iota(jnp.int32, (size, size), 1)
    diag = rows == cols
    work = gram
    made = jnp.where(diag, 1.0, 0.0).astype(F32)
    for k in range(size - 1):
        column = work[:, k : k + 1]
        factor = jnp.where(rows[:, :1] > k, column / work[k : k + 1, k : k + 1], 0.0)
        work, made = work - factor * work[k : k + 1, :], made - factor * made[k : k + 1, :]
    pivots = jnp.sum(jnp.where(diag, work, 0.0), axis=1, keepdims=True)
    return made * lax.rsqrt(pivots)


def kernel(
    n_row, n_col, turns,
    tiles_hbm, places, places_vec, counts, valid, start, rotations,
    maps_out, ritz_out,
    tiles, pick_rows, pick_cols, pick_half, direct, mirror, rows_total, cols_total,
    col_vecs, row_vecs, row_land, col_land, gram_row, gram_col,
    tile_sem, send_vec, recv_vec, send_sum, recv_sum, send_gram, recv_gram,
):
    me_row = lax.axis_index("row")
    me_col = lax.axis_index("col")
    slots, side, _ = tiles.shape
    count, stretch = start.shape
    per = stretch // side
    node_total = float(stretch * n_row * n_col)
    chunk = per * count

    fetch = pltpu.make_async_copy(tiles_hbm, tiles, tile_sem)
    fetch.start()

    def row_peer(d):
        return (lax.rem(me_row + d, n_row), me_col)

    def col_peer(d):
        return (me_row, lax.rem(me_col + d, n_col))

    peers = [("row", d) for d in range(1, n_row)] + [("col", d) for d in range(1, n_col)]
    barrier = pltpu.get_barrier_semaphore()
    for axis, d in peers:
        where = row_peer(d) if axis == "row" else col_peer(d)
        pl.semaphore_signal(barrier, inc=1, device_id=where, device_id_type=MESH)

    mask = valid[...].astype(F32)
    first = start[...] * mask

    def put_vectors(turn, top, bottom):
        both = jnp.concatenate([top, bottom], axis=0).astype(BF16)
        for k in range(per):
            part = both[:, k * side : (k + 1) * side]
            col_vecs[turn, me_row * per + k] = part
            row_vecs[turn, me_col * per + k] = part

    def vector_copies(turn):
        copies = []
        for at, (axis, d) in enumerate(peers):
            buffer, mine, where = (
                (col_vecs, me_row, row_peer(d)) if axis == "row" else (row_vecs, me_col, col_peer(d))
            )
            span = buffer.at[turn, pl.ds(mine * per, per)]
            copies.append(
                pltpu.make_async_remote_copy(
                    src_ref=span, dst_ref=span,
                    send_sem=send_vec.at[turn, at], recv_sem=recv_vec.at[turn, at],
                    device_id=where, device_id_type=MESH,
                )
            )
        return copies

    def sum_copies(turn, wide):
        copies = []
        height = chunk + (2 * count if wide else 0)
        for at, (axis, d) in enumerate(peers):
            total, land, there, where = (
                (cols_total, row_land, lax.rem(me_row + d, n_row), row_peer(d))
                if axis == "row"
                else (rows_total, col_land, lax.rem(me_col + d, n_col), col_peer(d))
            )
            copies.append(
                pltpu.make_async_remote_copy(
                    src_ref=total.at[turn, there, pl.ds(0, height)],
                    dst_ref=land.at[turn, d - 1, pl.ds(0, height)],
                    send_sem=send_sum.at[turn, at], recv_sem=recv_sum.at[turn, at],
                    device_id=where, device_id_type=MESH,
                )
            )
        return copies

    def gram_copies(turn, axis):
        copies = []
        for at, (name, d) in enumerate(peers):
            if name != axis:
                continue
            buffer, where = (gram_row, row_peer(d)) if axis == "row" else (gram_col, col_peer(d))
            copies.append(
                pltpu.make_async_remote_copy(
                    src_ref=buffer.at[turn, 0], dst_ref=buffer.at[turn, d],
                    send_sem=send_gram.at[turn, at], recv_sem=recv_gram.at[turn, at],
                    device_id=where, device_id_type=MESH,
                )
            )
        return copies

    started = []

    def begin(copies):
        for copy in copies:
            copy.start()
        started.extend(copies)
        return copies

    def arrive(copies):
        for copy in copies:
            copy.wait_recv()

    put_vectors(0, first, jnp.concatenate([mask, jnp.zeros((count - 1, stretch), F32)], axis=0))
    pl.semaphore_wait(barrier, len(peers))
    vec_moves = begin(vector_copies(0))

    spread = (
        lax.broadcasted_iota(jnp.int32, (slots, slots * count), 1) // count
        == lax.broadcasted_iota(jnp.int32, (slots, slots * count), 0)
    ).astype(F32).astype(BF16)
    at_rows = places_vec[0:1, :]
    at_cols = places_vec[1:2, :]
    slot_at = lax.broadcasted_iota(jnp.int32, (1, slots), 1)
    live = slot_at < counts[0, 0]
    whole_rows = me_row * (n_col * per) + at_rows
    whole_cols = (at_cols // per * n_col + me_col) * per + at_cols % per
    key_rows = jnp.where(live, at_rows, -1).astype(F32)
    key_cols = jnp.where(live & (whole_rows != whole_cols), at_cols, -1).astype(F32)
    weights = jnp.where(whole_rows != whole_cols, 1.0, 0.5).astype(F32)
    keys = [key_rows, key_cols, weights, jnp.zeros((13, slots), F32)]
    keys = jnp.concatenate(keys, axis=0).astype(BF16)
    wide_keys = jnp.dot(keys, spread, preferred_element_type=F32)
    lane = (lax.broadcasted_iota(jnp.int32, (1, slots * count), 1) % count).astype(F32)
    for pick, wide_key in ((pick_rows, wide_keys[0:1]), (pick_cols, wide_keys[1:2])):
        wanted = wide_key * float(count) + lane
        for low in range(0, pick.shape[0], 64):
            row_at = (lax.broadcasted_iota(jnp.int32, (64, slots * count), 0) + low).astype(F32)
            pick[pl.ds(low, 64), :] = (row_at == wanted).astype(F32).astype(BF16)

    def build_half():
        wanted = wide_keys[0:1] * float(count) + lane
        for low in range(0, pick_half.shape[0], 64):
            row_at = (lax.broadcasted_iota(jnp.int32, (64, slots * count), 0) + low).astype(F32)
            pick_half[pl.ds(low, 64), :] = jnp.where(row_at == wanted, wide_keys[2:3], 0.0).astype(BF16)

    def local_form(turn, vecs, scaled):
        def visit(step, carry):
            for more in range(0, UNROLL, 2):
                slot = step * UNROLL + more
                pair = tiles[pl.ds(slot, 2)].reshape(2 * side, side)
                by_col = [col_vecs[turn, places[1, slot + i]] for i in range(2)]
                forth = dot_lanes(jnp.concatenate(by_col, axis=0), pair)
                for i in range(2):
                    at = pl.multiple_of((slot + i) * count, count)
                    value = forth[2 * i * count : 2 * (i + 1) * count, i * side : (i + 1) * side]
                    direct[0, pl.ds(at, count), :] = value[:count] + value[count:]
            return carry

        lax.fori_loop(0, slots // UNROLL, visit, 0)
        high, low = split(direct[0])
        summed = jnp.dot(pick_half[...], high, preferred_element_type=F32)
        summed = summed + jnp.dot(pick_half[...], low, preferred_element_type=F32)
        blocks = summed.shape[0] // count
        left = [summed[p * count : (p + 1) * count] for p in range(blocks)]
        right = [row_vecs[turn, p].astype(F32) for p in range(blocks)]
        right = [value[:count] + value[count:] for value in right]
        left = jnp.concatenate(left + [-0.5 * scaled], axis=1)
        right = jnp.concatenate(right + [vecs], axis=1)
        both = jnp.concatenate([left, right], axis=0)
        cross = dot_lanes(both, both, lax.Precision.HIGHEST)
        return -(cross[:count, count:] + cross[count:, :count])

    def local_product(turn, wide):
        def visit(step, carry):
            for more in range(0, UNROLL, 2):
                slot = step * UNROLL + more
                pair = tiles[pl.ds(slot, 2)].reshape(2 * side, side)
                by_col = [col_vecs[turn, places[1, slot + i]] for i in range(2)]
                by_row = [row_vecs[turn, places[0, slot + i]] for i in range(2)]
                forth = dot_lanes(jnp.concatenate(by_col, axis=0), pair)
                back = jnp.dot(beside(*by_row), pair, preferred_element_type=F32)
                for i in range(2):
                    at = pl.multiple_of((slot + i) * count, count)
                    one = forth[2 * i * count : 2 * (i + 1) * count, i * side : (i + 1) * side]
                    two = back[2 * i * count : 2 * (i + 1) * count]
                    for terms, value in ((direct, one), (mirror, two)):
                        if wide:
                            terms[0, pl.ds(at, count), :] = value[:count]
                            terms[1, pl.ds(at, count), :] = value[count:]
                        else:
                            terms[0, pl.ds(at, count), :] = value[:count] + value[count:]
            return carry

        lax.fori_loop(0, slots // UNROLL, visit, 0)
        for pick, terms, total, groups in (
            (pick_cols, mirror, cols_total, n_row), (pick_rows, direct, rows_total, n_col)
        ):
            for half in range(2 if wide else 1):
                high, low = split(terms[half])
                summed = jnp.dot(pick[...], high, preferred_element_type=F32)
                summed = summed + jnp.dot(pick[...], low, preferred_element_type=F32)
                for group in range(groups):
                    part = summed[group * chunk : (group + 1) * chunk]
                    if half == 0:
                        total[turn, group, pl.ds(0, chunk), :] = part.astype(BF16)
                        continue
                    rows = jnp.concatenate(
                        [part[k * count : k * count + 1] for k in range(per)], axis=0
                    )
                    rest = rows - rows.astype(BF16).astype(F32)
                    fill = jnp.zeros((2 * count - 2 * per, side), F32)
                    rows = jnp.concatenate([rows, rest, fill], axis=0)
                    total[turn, group, pl.ds(chunk, 2 * count), :] = rows.astype(BF16)

    def gather_sums(turn, span):
        total = rows_total[turn, me_col, span, :].astype(F32)
        total = total + cols_total[turn, me_row, span, :].astype(F32)
        for d in range(1, n_col):
            total = total + col_land[turn, d - 1, span, :].astype(F32)
        for d in range(1, n_row):
            total = total + row_land[turn, d - 1, span, :].astype(F32)
        return total

    def collect(turn):
        total = gather_sums(turn, pl.ds(0, chunk))
        return jnp.concatenate([total[k * count : (k + 1) * count] for k in range(per)], axis=1)

    def collect_degree(turn):
        total = gather_sums(turn, pl.ds(chunk, 2 * count))
        total = total[:per] + total[per : 2 * per]
        return jnp.concatenate([total[k : k + 1] for k in range(per)], axis=1)

    def gram_send(turn, grams):
        gram_row[turn, 0] = jnp.zeros(gram_row.shape[2:], F32)
        gram_row[turn, 0, :, 0:count] = grams
        return begin(gram_copies(turn, "row"))

    def gram_begin(turn, vecs, images):
        both = jnp.concatenate([vecs, images], axis=0)
        return gram_send(turn, dot_lanes(both, vecs, lax.Precision.HIGHEST))

    def gram_cross(turn, moves):
        arrive(moves)
        total = jnp.zeros(gram_row.shape[2:], F32)
        for r in range(n_row):
            total = total + gram_row[turn, lax.rem(me_row - r + n_row, n_row)]
        gram_col[turn, 0] = total
        return begin(gram_copies(turn, "col"))

    def gram_end(turn, moves):
        arrive(moves)
        total = jnp.zeros(gram_col.shape[2:], F32)
        for c in range(n_col):
            total = total + gram_col[turn, lax.rem(me_col - c + n_col, n_col)]
        total = total / node_total
        inverse = inverse_lower(total[:count, :count])
        theta = dot_lanes(dot_high(inverse, total[count:, :count]), inverse, lax.Precision.HIGHEST)
        return inverse, theta

    fetch.wait()
    arrive(vec_moves)
    local_product(0, True)
    sum_moves = begin(sum_copies(0, True))
    build_half()
    arrive(sum_moves)
    degree = collect_degree(0)
    vecs, images = first, mask * (degree * first - collect(0))
    steps = step_images = None
    for turn in range(turns):
        high = images.astype(BF16).astype(F32)
        put_vectors(turn + 1, high, images - high)
        vec_moves = begin(vector_copies(turn + 1))
        gram_moves = gram_begin(turn, vecs, images)
        arrive(vec_moves)
        gram_moves = gram_cross(turn, gram_moves)
        last = turn == turns - 1
        scaled = degree * images
        if last:
            form = local_form(turn + 1, images, mask * scaled)
        else:
            local_product(turn + 1, False)
            sum_moves = begin(sum_copies(turn + 1, False))
        inverse, theta = gram_end(turn, gram_moves)
        pair = mix(inverse, jnp.concatenate([vecs, images], axis=1))
        turned = mix(theta, pair)
        rotation = rotations[turn]
        on_vecs, on_resid = rotation[:, :count], rotation[:, count : 2 * count]
        resid = pair[:, stretch:] - turned[:, :stretch]
        moved = mix(on_resid, jnp.concatenate([resid, -turned[:, stretch:]], axis=1))
        if steps is not None:
            old = mix(inverse, jnp.concatenate([steps, step_images], axis=1))
            moved = moved + mix(rotation[:, 2 * count :], old)
        kept = mix(on_vecs, pair)
        on_twice = mix(on_resid, inverse)
        steps = moved[:, :stretch]
        vecs = kept[:, :stretch] + steps
        if last:
            rest = moved[:, stretch:] + kept[:, stretch:]
            sides = jnp.concatenate([vecs, rest], axis=0)
            stack = jnp.concatenate([sides, mix(on_twice, images)], axis=0)
            known = dot_lanes(stack, sides, lax.Precision.HIGHEST)
            gram_x = known[:count, :count]
            gram_ax = known[count : 2 * count, :count] + known[2 * count :, count:]
            gram_ax = gram_ax + dot_lanes(mix(on_twice, form), on_twice, lax.Precision.HIGHEST)
            break
        arrive(sum_moves)
        twice = mask * (scaled - collect(turn + 1))
        step_images = moved[:, stretch:] + mix(on_twice, twice)
        images = kept[:, stretch:] + step_images
    gram_moves = gram_send(turns, jnp.concatenate([gram_x, gram_ax], axis=0))
    inverse, theta = gram_end(turns, gram_cross(turns, gram_moves))
    maps_out[...] = mix(inverse, vecs)
    ritz_out[...] = theta
    for copy in started:
        copy.wait_send()


def body(tiles, coords, counts, valid, start, rotations):
    n_row = lax.axis_size("row")
    n_col = lax.axis_size("col")
    slots, side = tiles.shape[2], tiles.shape[3]
    count, stretch = start.shape
    per = stretch // side
    turns = rotations.shape[0]
    phases = turns + 1
    chunk = per * count
    links = n_row + n_col - 2
    vmem = pl.BlockSpec(memory_space=pltpu.VMEM)
    smem = pl.BlockSpec(memory_space=pltpu.SMEM)
    places = coords.reshape(2, slots)
    return pl.pallas_call(
        functools.partial(kernel, n_row, n_col, turns),
        out_shape=(
            jax.ShapeDtypeStruct((count, stretch), F32),
            jax.ShapeDtypeStruct((count, count), F32),
        ),
        in_specs=[pl.BlockSpec(memory_space=pl.ANY), smem, vmem, smem, vmem, vmem, vmem],
        out_specs=(vmem, vmem),
        scratch_shapes=[
            pltpu.VMEM((slots, side, side), BF16),
            pltpu.VMEM((n_col * chunk, slots * count), BF16),
            pltpu.VMEM((n_row * chunk, slots * count), BF16),
            pltpu.VMEM((n_col * chunk, slots * count), BF16),
            pltpu.VMEM((2, slots * count, side), F32),
            pltpu.VMEM((2, slots * count, side), F32),
            pltpu.VMEM((turns, n_col, chunk + 2 * count, side), BF16),
            pltpu.VMEM((turns, n_row, chunk + 2 * count, side), BF16),
            pltpu.VMEM((phases, n_row * per, 2 * count, side), BF16),
            pltpu.VMEM((phases, n_col * per, 2 * count, side), BF16),
            pltpu.VMEM((turns, n_row - 1, chunk + 2 * count, side), BF16),
            pltpu.VMEM((turns, n_col - 1, chunk + 2 * count, side), BF16),
            pltpu.VMEM((phases, n_row, 2 * count, side), F32),
            pltpu.VMEM((phases, n_col, 2 * count, side), F32),
            pltpu.SemaphoreType.DMA(()),
        ]
        + [pltpu.SemaphoreType.DMA((phases, links))] * 2
        + [pltpu.SemaphoreType.DMA((turns, links))] * 2
        + [pltpu.SemaphoreType.DMA((phases, links))] * 2,
        compiler_params=pltpu.CompilerParams(
            collective_id=0, has_side_effects=True, vmem_limit_bytes=60 * 1024 * 1024
        ),
    )(
        tiles.reshape(slots, side, side), places, places, counts,
        valid.reshape(1, stretch), start, rotations,
    )


def solution(mesh):
    in_specs = (
        P("row", "col", None, None, None),
        P("row", "col", None, None),
        P("row", "col"),
        P(("row", "col")),
        P(None, ("row", "col")),
        P(),
    )
    out_specs = (P(None, ("row", "col")), P())
    return jax.shard_map(body, mesh=mesh, in_specs=in_specs, out_specs=out_specs, check_vma=False)
```

```python
import functools
import jax
import jax.numpy as jnp
from jax import lax
from jax.experimental import pallas as pl
from jax.experimental.pallas import tpu as pltpu
from jax.sharding import PartitionSpec as P

F32 = jnp.float32
BF16 = jnp.bfloat16
MESH = pl.DeviceIdType.MESH
UNROLL = 64


def dot_high(left, right):
    return jnp.dot(left, right, precision=lax.Precision.HIGHEST, preferred_element_type=F32)


def dot_lanes(left, right, precision=None):
    return lax.dot_general(
        left, right, (((1,), (1,)), ((), ())), precision=precision, preferred_element_type=F32
    )


def mix(left, right):
    total = left[:, 0:1] * right[0:1, :]
    for k in range(1, left.shape[1]):
        total = total + left[:, k : k + 1] * right[k : k + 1, :]
    return total


def beside(first, second):
    zero = jnp.zeros_like(first)
    return jnp.concatenate(
        [jnp.concatenate([first, zero], axis=1), jnp.concatenate([zero, second], axis=1)], axis=0
    )


def split(values):
    high = values.astype(BF16)
    return high, (values - high.astype(F32)).astype(BF16)


def inverse_lower(gram):
    size = gram.shape[0]
    rows = lax.broadcasted_iota(jnp.int32, (size, size), 0)
    cols = lax.broadcasted_iota(jnp.int32, (size, size), 1)
    diag = rows == cols
    work = gram
    made = jnp.where(diag, 1.0, 0.0).astype(F32)
    for k in range(size - 1):
        column = work[:, k : k + 1]
        factor = jnp.where(rows[:, :1] > k, column / work[k : k + 1, k : k + 1], 0.0)
        work, made = work - factor * work[k : k + 1, :], made - factor * made[k : k + 1, :]
    pivots = jnp.sum(jnp.where(diag, work, 0.0), axis=1, keepdims=True)
    return made * lax.rsqrt(pivots)


def kernel(
    n_row, n_col, turns,
    tiles_hbm, places, places_vec, counts, valid, start, rotations,
    maps_out, ritz_out,
    tiles, pick_rows, pick_cols, pick_half, direct, mirror, rows_total, cols_total,
    col_vecs, row_vecs, row_land, col_land, gram_row, gram_col,
    tile_sem, send_vec, recv_vec, send_sum, recv_sum, send_gram, recv_gram,
):
    me_row = lax.axis_index("row")
    me_col = lax.axis_index("col")
    slots, side, _ = tiles.shape
    count, stretch = start.shape
    per = stretch // side
    node_total = float(stretch * n_row * n_col)
    chunk = per * count

    fetch = pltpu.make_async_copy(tiles_hbm, tiles, tile_sem)
    fetch.start()

    def row_peer(d):
        return (lax.rem(me_row + d, n_row), me_col)

    def col_peer(d):
        return (me_row, lax.rem(me_col + d, n_col))

    peers = [("row", d) for d in range(1, n_row)] + [("col", d) for d in range(1, n_col)]
    barrier = pltpu.get_barrier_semaphore()
    for axis, d in peers:
        where = row_peer(d) if axis == "row" else col_peer(d)
        pl.semaphore_signal(barrier, inc=1, device_id=where, device_id_type=MESH)

    mask = valid[...].astype(F32)
    first = start[...] * mask

    def put_vectors(turn, top, bottom):
        both = jnp.concatenate([top, bottom], axis=0).astype(BF16)
        for k in range(per):
            part = both[:, k * side : (k + 1) * side]
            col_vecs[turn, me_row * per + k] = part
            row_vecs[turn, me_col * per + k] = part

    def vector_copies(turn):
        copies = []
        for at, (axis, d) in enumerate(peers):
            buffer, mine, where = (
                (col_vecs, me_row, row_peer(d)) if axis == "row" else (row_vecs, me_col, col_peer(d))
            )
            span = buffer.at[turn, pl.ds(mine * per, per)]
            copies.append(
                pltpu.make_async_remote_copy(
                    src_ref=span, dst_ref=span,
                    send_sem=send_vec.at[turn, at], recv_sem=recv_vec.at[turn, at],
                    device_id=where, device_id_type=MESH,
                )
            )
        return copies

    def sum_copies(turn, wide):
        copies = []
        height = chunk + (2 * count if wide else 0)
        for at, (axis, d) in enumerate(peers):
            total, land, there, where = (
                (cols_total, row_land, lax.rem(me_row + d, n_row), row_peer(d))
                if axis == "row"
                else (rows_total, col_land, lax.rem(me_col + d, n_col), col_peer(d))
            )
            copies.append(
                pltpu.make_async_remote_copy(
                    src_ref=total.at[turn, there, pl.ds(0, height)],
                    dst_ref=land.at[turn, d - 1, pl.ds(0, height)],
                    send_sem=send_sum.at[turn, at], recv_sem=recv_sum.at[turn, at],
                    device_id=where, device_id_type=MESH,
                )
            )
        return copies

    def gram_copies(turn, axis):
        copies = []
        for at, (name, d) in enumerate(peers):
            if name != axis:
                continue
            buffer, where = (gram_row, row_peer(d)) if axis == "row" else (gram_col, col_peer(d))
            copies.append(
                pltpu.make_async_remote_copy(
                    src_ref=buffer.at[turn, 0], dst_ref=buffer.at[turn, d],
                    send_sem=send_gram.at[turn, at], recv_sem=recv_gram.at[turn, at],
                    device_id=where, device_id_type=MESH,
                )
            )
        return copies

    started = []

    def begin(copies):
        for copy in copies:
            copy.start()
        started.extend(copies)
        return copies

    def arrive(copies):
        for copy in copies:
            copy.wait_recv()

    put_vectors(0, first, jnp.concatenate([mask, jnp.zeros((count - 1, stretch), F32)], axis=0))
    pl.semaphore_wait(barrier, len(peers))
    vec_moves = begin(vector_copies(0))

    spread = (
        lax.broadcasted_iota(jnp.int32, (slots, slots * count), 1) // count
        == lax.broadcasted_iota(jnp.int32, (slots, slots * count), 0)
    ).astype(F32).astype(BF16)
    at_rows = places_vec[0:1, :]
    at_cols = places_vec[1:2, :]
    slot_at = lax.broadcasted_iota(jnp.int32, (1, slots), 1)
    live = slot_at < counts[0, 0]
    whole_rows = me_row * (n_col * per) + at_rows
    whole_cols = (at_cols // per * n_col + me_col) * per + at_cols % per
    key_rows = jnp.where(live, at_rows, -1).astype(F32)
    key_cols = jnp.where(live & (whole_rows != whole_cols), at_cols, -1).astype(F32)
    weights = jnp.where(whole_rows != whole_cols, 1.0, 0.5).astype(F32)
    keys = [key_rows, key_cols, weights, jnp.zeros((13, slots), F32)]
    keys = jnp.concatenate(keys, axis=0).astype(BF16)
    wide_keys = jnp.dot(keys, spread, preferred_element_type=F32)
    lane = (lax.broadcasted_iota(jnp.int32, (1, slots * count), 1) % count).astype(F32)
    for pick, wide_key in ((pick_rows, wide_keys[0:1]), (pick_cols, wide_keys[1:2])):
        wanted = wide_key * float(count) + lane
        for low in range(0, pick.shape[0], 64):
            row_at = (lax.broadcasted_iota(jnp.int32, (64, slots * count), 0) + low).astype(F32)
            pick[pl.ds(low, 64), :] = (row_at == wanted).astype(F32).astype(BF16)

    def build_half():
        wanted = wide_keys[0:1] * float(count) + lane
        for low in range(0, pick_half.shape[0], 64):
            row_at = (lax.broadcasted_iota(jnp.int32, (64, slots * count), 0) + low).astype(F32)
            pick_half[pl.ds(low, 64), :] = jnp.where(row_at == wanted, wide_keys[2:3], 0.0).astype(BF16)

    def local_form(turn, vecs, scaled):
        def visit(step, carry):
            for more in range(0, UNROLL, 2):
                slot = step * UNROLL + more
                pair = tiles[pl.ds(slot, 2)].reshape(2 * side, side)
                by_col = [col_vecs[turn, places[1, slot + i]] for i in range(2)]
                forth = dot_lanes(jnp.concatenate(by_col, axis=0), pair)
                for i in range(2):
                    at = pl.multiple_of((slot + i) * count, count)
                    value = forth[2 * i * count : 2 * (i + 1) * count, i * side : (i + 1) * side]
                    direct[0, pl.ds(at, count), :] = value[:count] + value[count:]
            return carry

        lax.fori_loop(0, slots // UNROLL, visit, 0)
        high, low = split(direct[0])
        summed = jnp.dot(pick_half[...], high, preferred_element_type=F32)
        summed = summed + jnp.dot(pick_half[...], low, preferred_element_type=F32)
        blocks = summed.shape[0] // count
        left = [summed[p * count : (p + 1) * count] for p in range(blocks)]
        right = [row_vecs[turn, p].astype(F32) for p in range(blocks)]
        right = [value[:count] + value[count:] for value in right]
        left = jnp.concatenate(left + [-0.5 * scaled], axis=1)
        right = jnp.concatenate(right + [vecs], axis=1)
        both = jnp.concatenate([left, right], axis=0)
        cross = dot_lanes(both, both, lax.Precision.HIGHEST)
        return -(cross[:count, count:] + cross[count:, :count])

    def local_product(turn, wide):
        def visit(step, carry):
            for more in range(0, UNROLL, 2):
                slot = step * UNROLL + more
                pair = tiles[pl.ds(slot, 2)].reshape(2 * side, side)
                by_col = [col_vecs[turn, places[1, slot + i]] for i in range(2)]
                by_row = [row_vecs[turn, places[0, slot + i]] for i in range(2)]
                forth = dot_lanes(jnp.concatenate(by_col, axis=0), pair)
                back = jnp.dot(beside(*by_row), pair, preferred_element_type=F32)
                for i in range(2):
                    at = pl.multiple_of((slot + i) * count, count)
                    one = forth[2 * i * count : 2 * (i + 1) * count, i * side : (i + 1) * side]
                    two = back[2 * i * count : 2 * (i + 1) * count]
                    for terms, value in ((direct, one), (mirror, two)):
                        if wide:
                            terms[0, pl.ds(at, count), :] = value[:count]
                            terms[1, pl.ds(at, count), :] = value[count:]
                        else:
                            terms[0, pl.ds(at, count), :] = value[:count] + value[count:]
            return carry

        lax.fori_loop(0, slots // UNROLL, visit, 0)
        for pick, terms, total, groups in (
            (pick_cols, mirror, cols_total, n_row), (pick_rows, direct, rows_total, n_col)
        ):
            for half in range(2 if wide else 1):
                high, low = split(terms[half])
                summed = jnp.dot(pick[...], high, preferred_element_type=F32)
                summed = summed + jnp.dot(pick[...], low, preferred_element_type=F32)
                for group in range(groups):
                    part = summed[group * chunk : (group + 1) * chunk]
                    if half == 0:
                        total[turn, group, pl.ds(0, chunk), :] = part.astype(BF16)
                        continue
                    rows = jnp.concatenate(
                        [part[k * count : k * count + 1] for k in range(per)], axis=0
                    )
                    rest = rows - rows.astype(BF16).astype(F32)
                    fill = jnp.zeros((2 * count - 2 * per, side), F32)
                    rows = jnp.concatenate([rows, rest, fill], axis=0)
                    total[turn, group, pl.ds(chunk, 2 * count), :] = rows.astype(BF16)

    def gather_sums(turn, span):
        total = rows_total[turn, me_col, span, :].astype(F32)
        total = total + cols_total[turn, me_row, span, :].astype(F32)
        for d in range(1, n_col):
            total = total + col_land[turn, d - 1, span, :].astype(F32)
        for d in range(1, n_row):
            total = total + row_land[turn, d - 1, span, :].astype(F32)
        return total

    def collect(turn):
        total = gather_sums(turn, pl.ds(0, chunk))
        return jnp.concatenate([total[k * count : (k + 1) * count] for k in range(per)], axis=1)

    def collect_degree(turn):
        total = gather_sums(turn, pl.ds(chunk, 2 * count))
        total = total[:per] + total[per : 2 * per]
        return jnp.concatenate([total[k : k + 1] for k in range(per)], axis=1)

    def gram_send(turn, grams):
        gram_row[turn, 0] = jnp.zeros(gram_row.shape[2:], F32)
        gram_row[turn, 0, :, 0:count] = grams
        return begin(gram_copies(turn, "row"))

    def gram_begin(turn, vecs, images):
        both = jnp.concatenate([vecs, images], axis=0)
        return gram_send(turn, dot_lanes(both, vecs, lax.Precision.HIGHEST))

    def gram_cross(turn, moves):
        arrive(moves)
        total = jnp.zeros(gram_row.shape[2:], F32)
        for r in range(n_row):
            total = total + gram_row[turn, lax.rem(me_row - r + n_row, n_row)]
        gram_col[turn, 0] = total
        return begin(gram_copies(turn, "col"))

    def gram_end(turn, moves):
        arrive(moves)
        total = jnp.zeros(gram_col.shape[2:], F32)
        for c in range(n_col):
            total = total + gram_col[turn, lax.rem(me_col - c + n_col, n_col)]
        total = total / node_total
        inverse = inverse_lower(total[:count, :count])
        theta = dot_lanes(dot_high(inverse, total[count:, :count]), inverse, lax.Precision.HIGHEST)
        return inverse, theta

    fetch.wait()
    arrive(vec_moves)
    local_product(0, True)
    sum_moves = begin(sum_copies(0, True))
    build_half()
    arrive(sum_moves)
    degree = collect_degree(0)
    vecs, images = first, mask * (degree * first - collect(0))
    steps = step_images = None
    for turn in range(turns):
        high = images.astype(BF16).astype(F32)
        put_vectors(turn + 1, high, images - high)
        vec_moves = begin(vector_copies(turn + 1))
        gram_moves = gram_begin(turn, vecs, images)
        arrive(vec_moves)
        gram_moves = gram_cross(turn, gram_moves)
        last = turn == turns - 1
        scaled = degree * images
        if last:
            form = local_form(turn + 1, images, mask * scaled)
        else:
            local_product(turn + 1, False)
            sum_moves = begin(sum_copies(turn + 1, False))
        inverse, theta = gram_end(turn, gram_moves)
        pair = mix(inverse, jnp.concatenate([vecs, images], axis=1))
        turned = mix(theta, pair)
        rotation = rotations[turn]
        on_vecs, on_resid = rotation[:, :count], rotation[:, count : 2 * count]
        resid = pair[:, stretch:] - turned[:, :stretch]
        moved = mix(on_resid, jnp.concatenate([resid, -turned[:, stretch:]], axis=1))
        if steps is not None:
            old = mix(inverse, jnp.concatenate([steps, step_images], axis=1))
            moved = moved + mix(rotation[:, 2 * count :], old)
        kept = mix(on_vecs, pair)
        on_twice = mix(on_resid, inverse)
        steps = moved[:, :stretch]
        vecs = kept[:, :stretch] + steps
        if last:
            rest = moved[:, stretch:] + kept[:, stretch:]
            sides = jnp.concatenate([vecs, rest], axis=0)
            stack = jnp.concatenate([sides, mix(on_twice, images)], axis=0)
            known = dot_lanes(stack, sides, lax.Precision.HIGHEST)
            gram_x = known[:count, :count]
            gram_ax = known[count : 2 * count, :count] + known[2 * count :, count:]
            gram_ax = gram_ax + dot_lanes(mix(on_twice, form), on_twice, lax.Precision.HIGHEST)
            break
        arrive(sum_moves)
        twice = mask * (scaled - collect(turn + 1))
        step_images = moved[:, stretch:] + mix(on_twice, twice)
        images = kept[:, stretch:] + step_images
    gram_moves = gram_send(turns, jnp.concatenate([gram_x, gram_ax], axis=0))
    inverse, theta = gram_end(turns, gram_cross(turns, gram_moves))
    maps_out[...] = mix(inverse, vecs)
    ritz_out[...] = theta
    for copy in started:
        copy.wait_send()


def hand_out(maps_in, ritz_in, maps_out, ritz_out):
    maps_out[...] = maps_in[...]
    ritz_out[...] = ritz_in[...]


def body(tiles, coords, counts, valid, start, rotations):
    n_row = lax.axis_size("row")
    n_col = lax.axis_size("col")
    slots, side = tiles.shape[2], tiles.shape[3]
    count, stretch = start.shape
    per = stretch // side
    turns = rotations.shape[0]
    phases = turns + 1
    chunk = per * count
    links = n_row + n_col - 2
    vmem = pl.BlockSpec(memory_space=pltpu.VMEM)
    smem = pl.BlockSpec(memory_space=pltpu.SMEM)
    places = coords.reshape(2, slots)
    results = pl.pallas_call(
        functools.partial(kernel, n_row, n_col, turns),
        out_shape=(
            jax.ShapeDtypeStruct((count, stretch), F32),
            jax.ShapeDtypeStruct((count, count), F32),
        ),
        in_specs=[pl.BlockSpec(memory_space=pl.ANY), smem, vmem, smem, vmem, vmem, vmem],
        out_specs=(vmem, vmem),
        scratch_shapes=[
            pltpu.VMEM((slots, side, side), BF16),
            pltpu.VMEM((n_col * chunk, slots * count), BF16),
            pltpu.VMEM((n_row * chunk, slots * count), BF16),
            pltpu.VMEM((n_col * chunk, slots * count), BF16),
            pltpu.VMEM((2, slots * count, side), F32),
            pltpu.VMEM((2, slots * count, side), F32),
            pltpu.VMEM((turns, n_col, chunk + 2 * count, side), BF16),
            pltpu.VMEM((turns, n_row, chunk + 2 * count, side), BF16),
            pltpu.VMEM((phases, n_row * per, 2 * count, side), BF16),
            pltpu.VMEM((phases, n_col * per, 2 * count, side), BF16),
            pltpu.VMEM((turns, n_row - 1, chunk + 2 * count, side), BF16),
            pltpu.VMEM((turns, n_col - 1, chunk + 2 * count, side), BF16),
            pltpu.VMEM((phases, n_row, 2 * count, side), F32),
            pltpu.VMEM((phases, n_col, 2 * count, side), F32),
            pltpu.SemaphoreType.DMA(()),
        ]
        + [pltpu.SemaphoreType.DMA((phases, links))] * 2
        + [pltpu.SemaphoreType.DMA((turns, links))] * 2
        + [pltpu.SemaphoreType.DMA((phases, links))] * 2,
        compiler_params=pltpu.CompilerParams(
            collective_id=0, has_side_effects=True, vmem_limit_bytes=60 * 1024 * 1024
        ),
    )(
        tiles.reshape(slots, side, side), places, places, counts,
        valid.reshape(1, stretch), start, rotations,
    )
    return pl.pallas_call(
        hand_out,
        out_shape=tuple(jax.ShapeDtypeStruct(part.shape, part.dtype) for part in results),
        in_specs=[vmem, vmem],
        out_specs=(vmem, vmem),
    )(*results)


def solution(mesh):
    in_specs = (
        P("row", "col", None, None, None),
        P("row", "col", None, None),
        P("row", "col"),
        P(("row", "col")),
        P(None, ("row", "col")),
        P(),
    )
    out_specs = (P(None, ("row", "col")), P())
    return jax.shard_map(body, mesh=mesh, in_specs=in_specs, out_specs=out_specs, check_vma=False)
```

```python
import functools
import jax
import jax.numpy as jnp
from jax import lax
from jax.experimental import pallas as pl
from jax.experimental.pallas import tpu as pltpu
from jax.sharding import PartitionSpec as P

F32 = jnp.float32
BF16 = jnp.bfloat16
MESH = pl.DeviceIdType.MESH
UNROLL = 64


def dot_high(left, right):
    return jnp.dot(left, right, precision=lax.Precision.HIGHEST, preferred_element_type=F32)


def dot_lanes(left, right, precision=None):
    return lax.dot_general(
        left, right, (((1,), (1,)), ((), ())), precision=precision, preferred_element_type=F32
    )


def mix(left, right):
    total = left[:, 0:1] * right[0:1, :]
    for k in range(1, left.shape[1]):
        total = total + left[:, k : k + 1] * right[k : k + 1, :]
    return total


def beside(first, second):
    zero = jnp.zeros_like(first)
    return jnp.concatenate(
        [jnp.concatenate([first, zero], axis=1), jnp.concatenate([zero, second], axis=1)], axis=0
    )


def split(values):
    high = values.astype(BF16)
    return high, (values - high.astype(F32)).astype(BF16)


def inverse_lower(gram):
    size = gram.shape[0]
    rows = lax.broadcasted_iota(jnp.int32, (size, size), 0)
    cols = lax.broadcasted_iota(jnp.int32, (size, size), 1)
    diag = rows == cols
    work = gram
    made = jnp.where(diag, 1.0, 0.0).astype(F32)
    for k in range(size - 1):
        column = work[:, k : k + 1]
        factor = jnp.where(rows[:, :1] > k, column / work[k : k + 1, k : k + 1], 0.0)
        work, made = work - factor * work[k : k + 1, :], made - factor * made[k : k + 1, :]
    pivots = jnp.sum(jnp.where(diag, work, 0.0), axis=1, keepdims=True)
    return made * lax.rsqrt(pivots)


def kernel(
    n_row, n_col, turns,
    tiles_hbm, places, places_vec, counts, valid, start, rotations,
    maps_out, ritz_out,
    tiles, pick_rows, pick_cols, pick_half, direct, mirror, rows_total, cols_total,
    col_vecs, row_vecs, row_land, col_land, gram_row, gram_col,
    tile_sem, send_vec, recv_vec, send_sum, recv_sum, send_gram, recv_gram,
):
    me_row = lax.axis_index("row")
    me_col = lax.axis_index("col")
    slots, side, _ = tiles.shape
    count, stretch = start.shape
    per = stretch // side
    node_total = float(stretch * n_row * n_col)
    chunk = per * count

    fetch = pltpu.make_async_copy(tiles_hbm, tiles, tile_sem)
    fetch.start()

    def row_peer(d):
        return (lax.rem(me_row + d, n_row), me_col)

    def col_peer(d):
        return (me_row, lax.rem(me_col + d, n_col))

    peers = [("row", d) for d in range(1, n_row)] + [("col", d) for d in range(1, n_col)]
    barrier = pltpu.get_barrier_semaphore()
    for axis, d in peers:
        where = row_peer(d) if axis == "row" else col_peer(d)
        pl.semaphore_signal(barrier, inc=1, device_id=where, device_id_type=MESH)

    mask = valid[...].astype(F32)
    first = start[...] * mask

    def put_vectors(turn, top, bottom):
        both = jnp.concatenate([top, bottom], axis=0).astype(BF16)
        for k in range(per):
            part = both[:, k * side : (k + 1) * side]
            col_vecs[turn, me_row * per + k] = part
            row_vecs[turn, me_col * per + k] = part

    def vector_copies(turn):
        copies = []
        for at, (axis, d) in enumerate(peers):
            buffer, mine, where = (
                (col_vecs, me_row, row_peer(d)) if axis == "row" else (row_vecs, me_col, col_peer(d))
            )
            span = buffer.at[turn, pl.ds(mine * per, per)]
            copies.append(
                pltpu.make_async_remote_copy(
                    src_ref=span, dst_ref=span,
                    send_sem=send_vec.at[turn, at], recv_sem=recv_vec.at[turn, at],
                    device_id=where, device_id_type=MESH,
                )
            )
        return copies

    def sum_copies(turn, wide):
        copies = []
        height = chunk + (2 * count if wide else 0)
        for at, (axis, d) in enumerate(peers):
            total, land, there, where = (
                (cols_total, row_land, lax.rem(me_row + d, n_row), row_peer(d))
                if axis == "row"
                else (rows_total, col_land, lax.rem(me_col + d, n_col), col_peer(d))
            )
            copies.append(
                pltpu.make_async_remote_copy(
                    src_ref=total.at[turn, there, pl.ds(0, height)],
                    dst_ref=land.at[turn, d - 1, pl.ds(0, height)],
                    send_sem=send_sum.at[turn, at], recv_sem=recv_sum.at[turn, at],
                    device_id=where, device_id_type=MESH,
                )
            )
        return copies

    def gram_copies(turn, axis):
        copies = []
        for at, (name, d) in enumerate(peers):
            if name != axis:
                continue
            buffer, where = (gram_row, row_peer(d)) if axis == "row" else (gram_col, col_peer(d))
            copies.append(
                pltpu.make_async_remote_copy(
                    src_ref=buffer.at[turn, 0], dst_ref=buffer.at[turn, d],
                    send_sem=send_gram.at[turn, at], recv_sem=recv_gram.at[turn, at],
                    device_id=where, device_id_type=MESH,
                )
            )
        return copies

    started = []

    def begin(copies):
        for copy in copies:
            copy.start()
        started.extend(copies)
        return copies

    def arrive(copies):
        for copy in copies:
            copy.wait_recv()

    put_vectors(0, first, jnp.concatenate([mask, jnp.zeros((count - 1, stretch), F32)], axis=0))
    pl.semaphore_wait(barrier, len(peers))
    vec_moves = begin(vector_copies(0))

    spread = (
        lax.broadcasted_iota(jnp.int32, (slots, slots * count), 1) // count
        == lax.broadcasted_iota(jnp.int32, (slots, slots * count), 0)
    ).astype(F32).astype(BF16)
    at_rows = places_vec[0:1, :]
    at_cols = places_vec[1:2, :]
    slot_at = lax.broadcasted_iota(jnp.int32, (1, slots), 1)
    live = slot_at < counts[0, 0]
    whole_rows = me_row * (n_col * per) + at_rows
    whole_cols = (at_cols // per * n_col + me_col) * per + at_cols % per
    key_rows = jnp.where(live, at_rows, -1).astype(F32)
    key_cols = jnp.where(live & (whole_rows != whole_cols), at_cols, -1).astype(F32)
    weights = jnp.where(whole_rows != whole_cols, 1.0, 0.5).astype(F32)
    keys = [key_rows, key_cols, weights, jnp.zeros((13, slots), F32)]
    keys = jnp.concatenate(keys, axis=0).astype(BF16)
    wide_keys = jnp.dot(keys, spread, preferred_element_type=F32)
    lane = (lax.broadcasted_iota(jnp.int32, (1, slots * count), 1) % count).astype(F32)
    for pick, wide_key in ((pick_rows, wide_keys[0:1]), (pick_cols, wide_keys[1:2])):
        wanted = wide_key * float(count) + lane
        for low in range(0, pick.shape[0], 64):
            row_at = (lax.broadcasted_iota(jnp.int32, (64, slots * count), 0) + low).astype(F32)
            pick[pl.ds(low, 64), :] = (row_at == wanted).astype(F32).astype(BF16)

    def build_half():
        wanted = wide_keys[0:1] * float(count) + lane
        for low in range(0, pick_half.shape[0], 64):
            row_at = (lax.broadcasted_iota(jnp.int32, (64, slots * count), 0) + low).astype(F32)
            pick_half[pl.ds(low, 64), :] = jnp.where(row_at == wanted, wide_keys[2:3], 0.0).astype(BF16)

    def local_form(turn, vecs, scaled):
        def visit(step, carry):
            for more in range(0, UNROLL, 2):
                slot = step * UNROLL + more
                pair = tiles[pl.ds(slot, 2)].reshape(2 * side, side)
                by_col = [col_vecs[turn, places[1, slot + i]] for i in range(2)]
                forth = dot_lanes(jnp.concatenate(by_col, axis=0), pair)
                for i in range(2):
                    at = pl.multiple_of((slot + i) * count, count)
                    value = forth[2 * i * count : 2 * (i + 1) * count, i * side : (i + 1) * side]
                    direct[0, pl.ds(at, count), :] = value[:count] + value[count:]
            return carry

        lax.fori_loop(0, slots // UNROLL, visit, 0)
        high, low = split(direct[0])
        summed = jnp.dot(pick_half[...], high, preferred_element_type=F32)
        summed = summed + jnp.dot(pick_half[...], low, preferred_element_type=F32)
        blocks = summed.shape[0] // count
        left = [summed[p * count : (p + 1) * count] for p in range(blocks)]
        right = [row_vecs[turn, p].astype(F32) for p in range(blocks)]
        right = [value[:count] + value[count:] for value in right]
        left = jnp.concatenate(left + [-0.5 * scaled], axis=1)
        right = jnp.concatenate(right + [vecs], axis=1)
        both = jnp.concatenate([left, right], axis=0)
        cross = dot_lanes(both, both, lax.Precision.HIGHEST)
        return -(cross[:count, count:] + cross[count:, :count])

    def local_product(turn, wide):
        def visit(step, carry):
            for more in range(0, UNROLL, 2):
                slot = step * UNROLL + more
                pair = tiles[pl.ds(slot, 2)].reshape(2 * side, side)
                by_col = [col_vecs[turn, places[1, slot + i]] for i in range(2)]
                by_row = [row_vecs[turn, places[0, slot + i]] for i in range(2)]
                forth = dot_lanes(jnp.concatenate(by_col, axis=0), pair)
                back = jnp.dot(beside(*by_row), pair, preferred_element_type=F32)
                for i in range(2):
                    at = pl.multiple_of((slot + i) * count, count)
                    one = forth[2 * i * count : 2 * (i + 1) * count, i * side : (i + 1) * side]
                    two = back[2 * i * count : 2 * (i + 1) * count]
                    for terms, value in ((direct, one), (mirror, two)):
                        if wide:
                            terms[0, pl.ds(at, count), :] = value[:count]
                            terms[1, pl.ds(at, count), :] = value[count:]
                        else:
                            terms[0, pl.ds(at, count), :] = value[:count] + value[count:]
            return carry

        lax.fori_loop(0, slots // UNROLL, visit, 0)
        for pick, terms, total, groups in (
            (pick_cols, mirror, cols_total, n_row), (pick_rows, direct, rows_total, n_col)
        ):
            for half in range(2 if wide else 1):
                high, low = split(terms[half])
                summed = jnp.dot(pick[...], high, preferred_element_type=F32)
                summed = summed + jnp.dot(pick[...], low, preferred_element_type=F32)
                for group in range(groups):
                    part = summed[group * chunk : (group + 1) * chunk]
                    if half == 0:
                        total[turn, group, pl.ds(0, chunk), :] = part.astype(BF16)
                        continue
                    rows = jnp.concatenate(
                        [part[k * count : k * count + 1] for k in range(per)], axis=0
                    )
                    rest = rows - rows.astype(BF16).astype(F32)
                    fill = jnp.zeros((2 * count - 2 * per, side), F32)
                    rows = jnp.concatenate([rows, rest, fill], axis=0)
                    total[turn, group, pl.ds(chunk, 2 * count), :] = rows.astype(BF16)

    def gather_sums(turn, span):
        total = rows_total[turn, me_col, span, :].astype(F32)
        total = total + cols_total[turn, me_row, span, :].astype(F32)
        for d in range(1, n_col):
            total = total + col_land[turn, d - 1, span, :].astype(F32)
        for d in range(1, n_row):
            total = total + row_land[turn, d - 1, span, :].astype(F32)
        return total

    def collect(turn):
        total = gather_sums(turn, pl.ds(0, chunk))
        return jnp.concatenate([total[k * count : (k + 1) * count] for k in range(per)], axis=1)

    def collect_degree(turn):
        total = gather_sums(turn, pl.ds(chunk, 2 * count))
        total = total[:per] + total[per : 2 * per]
        return jnp.concatenate([total[k : k + 1] for k in range(per)], axis=1)

    def gram_send(turn, grams):
        gram_row[turn, 0] = jnp.zeros(gram_row.shape[2:], F32)
        gram_row[turn, 0, 0 : grams.shape[0], 0 : grams.shape[1]] = grams
        return begin(gram_copies(turn, "row"))

    def gram_begin(turn, vecs, images):
        both = jnp.concatenate([vecs, images], axis=0)
        return gram_send(turn, dot_lanes(both, vecs, lax.Precision.HIGHEST))

    def gram_cross(turn, moves):
        arrive(moves)
        total = jnp.zeros(gram_row.shape[2:], F32)
        for r in range(n_row):
            total = total + gram_row[turn, lax.rem(me_row - r + n_row, n_row)]
        gram_col[turn, 0] = total
        return begin(gram_copies(turn, "col"))

    def gram_end(turn, moves):
        arrive(moves)
        total = jnp.zeros(gram_col.shape[2:], F32)
        for c in range(n_col):
            total = total + gram_col[turn, lax.rem(me_col - c + n_col, n_col)]
        return total / node_total

    def congruence(left, inner):
        return dot_lanes(dot_high(left, inner), left, lax.Precision.HIGHEST)

    def settle_small(total):
        inverse = inverse_lower(total[:count, :count])
        return inverse, congruence(inverse, total[count : 2 * count, :count])

    fetch.wait()
    arrive(vec_moves)
    local_product(0, True)
    sum_moves = begin(sum_copies(0, True))
    build_half()
    arrive(sum_moves)
    degree = collect_degree(0)
    vecs, images = first, mask * (degree * first - collect(0))
    steps = step_images = None
    for turn in range(turns):
        high = images.astype(BF16).astype(F32)
        put_vectors(turn + 1, high, images - high)
        vec_moves = begin(vector_copies(turn + 1))
        last = turn == turns - 1
        scaled = degree * images
        if last:
            basis = jnp.concatenate([vecs, images, steps, step_images], axis=0)
            gram_moves = gram_send(turn, dot_lanes(basis, basis, lax.Precision.HIGHEST))
            arrive(vec_moves)
            gram_moves = gram_cross(turn, gram_moves)
            form = local_form(turn + 1, images, mask * scaled)
            break
        gram_moves = gram_begin(turn, vecs, images)
        arrive(vec_moves)
        gram_moves = gram_cross(turn, gram_moves)
        local_product(turn + 1, False)
        sum_moves = begin(sum_copies(turn + 1, False))
        inverse, theta = settle_small(gram_end(turn, gram_moves))
        pair = mix(inverse, jnp.concatenate([vecs, images], axis=1))
        turned = mix(theta, pair)
        rotation = rotations[turn]
        on_vecs, on_resid = rotation[:, :count], rotation[:, count : 2 * count]
        resid = pair[:, stretch:] - turned[:, :stretch]
        moved = mix(on_resid, jnp.concatenate([resid, -turned[:, stretch:]], axis=1))
        if steps is not None:
            old = mix(inverse, jnp.concatenate([steps, step_images], axis=1))
            moved = moved + mix(rotation[:, 2 * count :], old)
        kept = mix(on_vecs, pair)
        on_twice = mix(on_resid, inverse)
        steps = moved[:, :stretch]
        vecs = kept[:, :stretch] + steps
        arrive(sum_moves)
        twice = mask * (scaled - collect(turn + 1))
        step_images = moved[:, stretch:] + mix(on_twice, twice)
        images = kept[:, stretch:] + step_images
    form_moves = gram_send(turns, form)
    total = gram_end(turns - 1, gram_moves)[:, : 4 * count]
    inverse, theta = settle_small(total)
    rotation = rotations[turns - 1]
    on_vecs, on_resid = rotation[:, :count], rotation[:, count : 2 * count]
    on_resid, on_steps = mix(on_resid, inverse), mix(rotation[:, 2 * count :], inverse)
    on_vecs = mix(on_vecs - mix(rotation[:, count : 2 * count], theta), inverse)
    zero = jnp.zeros_like(inverse)
    on_basis = jnp.concatenate([on_vecs, on_resid, on_steps, zero], axis=1)
    on_rest = jnp.concatenate([zero, on_vecs, zero, on_steps], axis=1)
    form_moves = gram_cross(turns, form_moves)
    sides = dot_high(jnp.concatenate([on_basis, on_rest], axis=0), total)
    sides = dot_lanes(sides, on_basis, lax.Precision.HIGHEST)
    crossed = mix(on_resid, total[count : 2 * count])
    known = sides[count:] + dot_lanes(crossed, on_rest, lax.Precision.HIGHEST)
    inverse = inverse_lower(sides[:count])
    known = congruence(inverse, known)
    outer = mix(inverse, on_resid)
    maps = mix(on_vecs, vecs) + mix(on_resid, images) + mix(on_steps, steps)
    maps_out[...] = mix(inverse, maps)
    form = gram_end(turns, form_moves)[:count, :count]
    ritz_out[...] = known + congruence(outer, form)
    for copy in started:
        copy.wait_send()


def hand_out(maps_in, ritz_in, maps_out, ritz_out):
    maps_out[...] = maps_in[...]
    ritz_out[...] = ritz_in[...]


def body(tiles, coords, counts, valid, start, rotations):
    n_row = lax.axis_size("row")
    n_col = lax.axis_size("col")
    slots, side = tiles.shape[2], tiles.shape[3]
    count, stretch = start.shape
    per = stretch // side
    turns = rotations.shape[0]
    phases = turns + 1
    chunk = per * count
    links = n_row + n_col - 2
    vmem = pl.BlockSpec(memory_space=pltpu.VMEM)
    smem = pl.BlockSpec(memory_space=pltpu.SMEM)
    places = coords.reshape(2, slots)
    results = pl.pallas_call(
        functools.partial(kernel, n_row, n_col, turns),
        out_shape=(
            jax.ShapeDtypeStruct((count, stretch), F32),
            jax.ShapeDtypeStruct((count, count), F32),
        ),
        in_specs=[pl.BlockSpec(memory_space=pl.ANY), smem, vmem, smem, vmem, vmem, vmem],
        out_specs=(vmem, vmem),
        scratch_shapes=[
            pltpu.VMEM((slots, side, side), BF16),
            pltpu.VMEM((n_col * chunk, slots * count), BF16),
            pltpu.VMEM((n_row * chunk, slots * count), BF16),
            pltpu.VMEM((n_col * chunk, slots * count), BF16),
            pltpu.VMEM((2, slots * count, side), F32),
            pltpu.VMEM((2, slots * count, side), F32),
            pltpu.VMEM((turns, n_col, chunk + 2 * count, side), BF16),
            pltpu.VMEM((turns, n_row, chunk + 2 * count, side), BF16),
            pltpu.VMEM((phases, n_row * per, 2 * count, side), BF16),
            pltpu.VMEM((phases, n_col * per, 2 * count, side), BF16),
            pltpu.VMEM((turns, n_row - 1, chunk + 2 * count, side), BF16),
            pltpu.VMEM((turns, n_col - 1, chunk + 2 * count, side), BF16),
            pltpu.VMEM((phases, n_row, 4 * count, side), F32),
            pltpu.VMEM((phases, n_col, 4 * count, side), F32),
            pltpu.SemaphoreType.DMA(()),
        ]
        + [pltpu.SemaphoreType.DMA((phases, links))] * 2
        + [pltpu.SemaphoreType.DMA((turns, links))] * 2
        + [pltpu.SemaphoreType.DMA((phases, links))] * 2,
        compiler_params=pltpu.CompilerParams(
            collective_id=0, has_side_effects=True, vmem_limit_bytes=60 * 1024 * 1024
        ),
    )(
        tiles.reshape(slots, side, side), places, places, counts,
        valid.reshape(1, stretch), start, rotations,
    )
    return pl.pallas_call(
        hand_out,
        out_shape=tuple(jax.ShapeDtypeStruct(part.shape, part.dtype) for part in results),
        in_specs=[vmem, vmem],
        out_specs=(vmem, vmem),
    )(*results)


def solution(mesh):
    in_specs = (
        P("row", "col", None, None, None),
        P("row", "col", None, None),
        P("row", "col"),
        P(("row", "col")),
        P(None, ("row", "col")),
        P(),
    )
    out_specs = (P(None, ("row", "col")), P())
    return jax.shard_map(body, mesh=mesh, in_specs=in_specs, out_specs=out_specs, check_vma=False)
```
